32 devices in a mesh: parts: 2 (over x), shard: 4 (over y, core), sub: 4 (over z).
Axes of the slice: x: 2, y: 2, z: 4, core: 2. Of those that a mesh axis runs over, the one named last changes fastest.
Arguments:
- host_factors: float32 [8192, 256], P(('parts', 'shard', 'sub')), parts along dimension 0, may hold values from -6 to 6
- token_ids: int32 [8192, 16], P(('parts', 'shard', 'sub')), parts along dimension 0, may hold values from 0 to 131071, as said below
- counts: int32 [8192, 16], P(('parts', 'shard', 'sub')), parts along dimension 0, may hold values from 1 to 63
- lengths: int32 [8192], P(('parts', 'shard', 'sub')), parts along dimension 0, may hold values from 2 to 16
- token_factors: bfloat16 [262144, 256], P(('parts', 'shard', 'sub')), parts along dimension 0, as said below
Outputs:
- new_factors: float32 [8192, 256], P(('parts', 'shard', 'sub')), parts along dimension 0
The draws below stay inside these ranges and needn't reach their ends.
There are 2 independent parts, one for each index of `parts`. The reference program is written for one: setup_inputs(seed, part) draws one part's arguments, and reference() takes and returns one part's arrays. A program takes and returns all parts, laid end to end along the dimension named above; each array names one. Nothing has to cross between parts.
Inputs may be any that keep to these rules, and one draw needn't show every extreme that they name: `token_ids`: token id t belongs to the device t // 8192 along shard+sub. Among the live slots of one device's 256 hosts, at most 256 name tokens of any one owner, and in every draw some owner is named exactly 256 times by each device's live slots. `token_factors`: factors of order one over the square root of the token count.
All inputs are finite; a program needn't handle non-finite values.
Results may differ from the reference program's by a relative error of at most 0.0003.
Values may be sent and summed in bfloat16 or wider, within the bound.
A program may use at most 64 MiB of HBM per device.

```python
import math
import jax
import jax.numpy as jnp
from jax import lax

FACTOR_DIM = 256
HOST_DEV = 256
SLOTS = 16
TOK_DEV = 8192
CG_STEPS = 3
CAPACITY = 256
ALL_HOSTS = 4096
ALL_TOKENS = 131072


def shared_layout(key):
    device_count = ALL_HOSTS // HOST_DEV
    key_length, key_favour, key_score, key_padding, key_local, key_shuffle = jax.random.split(key, 6)
    virtual_lengths = jax.random.randint(key_length, (device_count, HOST_DEV), 2, SLOTS + 1)
    alive_mask = jnp.arange(SLOTS)[None, None, :] < virtual_lengths[:, :, None]
    flat_alive = alive_mask.reshape(device_count, HOST_DEV * SLOTS).astype(jnp.int32)
    ordinal = jnp.cumsum(flat_alive, axis=1) - 1
    favoured = jax.random.randint(key_favour, (device_count, 1), 0, device_count)
    repeated = jnp.broadcast_to((jnp.arange(device_count * CAPACITY) // CAPACITY)[None, :], (device_count, device_count * CAPACITY))
    priority = jax.random.randint(key_score, (device_count, device_count * CAPACITY), 0, 1 << 20)
    priority = jnp.where(repeated == favoured, -1, priority)
    arrangement = jnp.argsort(priority, axis=1, stable=True)
    listing = jnp.take_along_axis(repeated, arrangement, 1)
    owner_alive = jnp.take_along_axis(listing, jnp.clip(ordinal, 0, device_count * CAPACITY - 1), 1)
    owner_padding = jax.random.randint(key_padding, (device_count, HOST_DEV * SLOTS), 0, device_count)
    owners = jnp.where(flat_alive > 0, owner_alive, owner_padding)
    local_rows = jax.random.randint(key_local, (device_count, HOST_DEV * SLOTS), 0, TOK_DEV)
    identities = (owners * TOK_DEV + local_rows).reshape(device_count, HOST_DEV, SLOTS)
    shuffle = jnp.argsort(jax.random.randint(key_shuffle, (device_count, HOST_DEV), 0, 1 << 24), axis=1, stable=True)
    identities = jnp.take_along_axis(identities, shuffle[:, :, None], 1)
    shuffled_lengths = jnp.take_along_axis(virtual_lengths, shuffle, 1)
    return (identities.reshape(ALL_HOSTS, SLOTS).astype(jnp.int32), shuffled_lengths.reshape(ALL_HOSTS).astype(jnp.int32))


def draw_token_ids(key, part):
    identities, shuffled_lengths = shared_layout(key)
    return identities


def draw_lengths(key, part):
    identities, shuffled_lengths = shared_layout(key)
    return shuffled_lengths


def draw_token_factors(key, part):
    key = jax.random.fold_in(key, 11)
    key_values, key_rows, key_columns = jax.random.split(key, 3)
    values = jax.random.normal(key_values, (ALL_TOKENS, FACTOR_DIM), jnp.float32)
    row_scale = jnp.exp(jax.random.uniform(key_rows, (ALL_TOKENS, 1), jnp.float32, 0.0, math.log(10.0)))
    column_scale = jnp.exp(jax.random.uniform(key_columns, (1, FACTOR_DIM), jnp.float32, math.log(0.3), math.log(3.0)))
    factor = 1.0 / (4.0 * math.sqrt(ALL_TOKENS))
    return (values * row_scale * column_scale * factor).astype(jnp.bfloat16)


def set_ends(entries, own_key, least, high):
    index_at = [jax.random.randint(jax.random.fold_in(own_key, axis), (), 0, length) for axis, length in enumerate(entries.shape)]
    longest = entries.shape.index(max(entries.shape))
    neighbour = index_at[:longest] + [(index_at[longest] + 1) % entries.shape[longest]] + index_at[longest + 1:]
    return entries.at[tuple(index_at)].set(least).at[tuple(neighbour)].set(high)


def levels(stream_key, dims, shards, low, high):
    gain, own = 1.0, jax.random.fold_in(stream_key, 6)
    for dim, shards_of in shards:
        draws = jnp.exp(jax.random.uniform(jax.random.fold_in(own, dim), (shards_of,), jnp.float32, low / len(shards), high / len(shards)))
        gain = gain * jnp.repeat(draws, dims[dim] // shards_of).reshape([-1 if axis == dim else 1 for axis in range(len(dims))])
    return gain


def centred(key, shape, spread, most, pieces=(), kind=jnp.bfloat16):
    level = levels(key, shape, pieces, -0.22, 0.18) if pieces else 1.0
    drawn = jax.random.normal(key, shape, jnp.float32) * spread * level
    return jnp.minimum(jnp.maximum(drawn, -most), most).astype(kind)


def setup_inputs(seed: int = 0, part: int = 0) -> dict:
    key_list = jax.random.split(jax.random.key(seed), 6)
    own_keys = jax.random.split(jax.random.fold_in(key_list[5], part), 6)
    return {
        "host_factors": centred(own_keys[0], (ALL_HOSTS, FACTOR_DIM), 1.0, 6.0, ((0, 16),), jnp.float32),
        "token_ids": draw_token_ids(jax.random.fold_in(jax.random.fold_in(key_list[5], part), 71), part),
        "counts": set_ends(jax.random.randint(own_keys[2], (ALL_HOSTS, SLOTS), 1, 64), jax.random.fold_in(own_keys[2], 1), 1, 63).astype(jnp.int32),
        "lengths": draw_lengths(jax.random.fold_in(jax.random.fold_in(key_list[5], part), 71), part),
        "token_factors": draw_token_factors(jax.random.fold_in(jax.random.fold_in(key_list[5], part), 71), part),
    }


CONFIDENCE_SCALE = 40.0
RIDGE_WEIGHT = 0.1
SMALL_EPSILON = 1e-6
HIGHEST = lax.Precision.HIGHEST


def system_product(gram_matrix, gathered, weights, vectors):
    projected = jnp.einsum("hsr,hr->hs", gathered, vectors, precision=HIGHEST, preferred_element_type=jnp.float32)
    spread_back = jnp.einsum("hsr,hs->hr", gathered, weights * projected, precision=HIGHEST, preferred_element_type=jnp.float32)
    return jnp.dot(vectors, gram_matrix, precision=HIGHEST) + RIDGE_WEIGHT * vectors + spread_back


def conjugate_steps(gram_matrix, gathered, block_counts, alive, start_point):
    scaled = CONFIDENCE_SCALE * block_counts.astype(jnp.float32)
    weights = jnp.where(alive, scaled, jnp.zeros_like(scaled))
    targets = jnp.where(alive, 1.0 + scaled, jnp.zeros_like(scaled))
    target_sum = jnp.einsum("hsr,hs->hr", gathered, targets, precision=HIGHEST, preferred_element_type=jnp.float32)
    iterate = start_point
    residual = target_sum - system_product(gram_matrix, gathered, weights, iterate)
    direction = residual
    norm_now = jnp.sum(residual * residual, axis=1, keepdims=True)
    for iteration in range(CG_STEPS):
        image = system_product(gram_matrix, gathered, weights, direction)
        step_size = norm_now / (jnp.sum(direction * image, axis=1, keepdims=True) + SMALL_EPSILON)
        iterate = iterate + step_size * direction
        residual = residual - step_size * image
        norm_next = jnp.sum(residual * residual, axis=1, keepdims=True)
        direction = residual + (norm_next / (norm_now + SMALL_EPSILON)) * direction
        norm_now = norm_next
    return iterate


def reference(host_factors, token_ids, counts, lengths, token_factors):
    gram_matrix = lax.dot_general(token_factors, token_factors, (((0,), (0,)), ((), ())), preferred_element_type=jnp.float32)
    blocks = ALL_HOSTS // HOST_DEV

    def solve_block(packed):
        start_point, block_ids, block_counts, block_lengths = packed
        alive = jnp.arange(SLOTS, dtype=jnp.int32)[None, :] < block_lengths[:, None]
        gathered = token_factors[block_ids]
        return conjugate_steps(gram_matrix, gathered, block_counts, alive, start_point)

    solved = lax.map(solve_block, (host_factors.reshape(blocks, HOST_DEV, FACTOR_DIM), token_ids.reshape(blocks, HOST_DEV, SLOTS), counts.reshape(blocks, HOST_DEV, SLOTS), lengths.reshape(blocks, HOST_DEV)))
    return solved.reshape(ALL_HOSTS, FACTOR_DIM)
```

```python
import functools
import math

import jax
import jax.numpy as jnp
from jax import lax
from jax.experimental import pallas as pl
from jax.experimental.pallas import tpu as pltpu
from jax.sharding import PartitionSpec as P

CG_STEPS = 3
CONFIDENCE_SCALE = 40.0
RIDGE_WEIGHT = 0.1
SMALL_EPSILON = 1e-06
HIGHEST = lax.Precision.HIGHEST
COUNT_SPAN = 64


def owner_ranks(owner_hot, block_rows):
    total_rows, owner_width = owner_hot.shape
    block_count = total_rows // block_rows
    blocked = owner_hot.reshape(block_count, block_rows, owner_width)
    position = jnp.arange(block_rows, dtype=jnp.int32)
    lower_mask = (position[:, None] > position[None, :]).astype(jnp.bfloat16)
    within = jnp.einsum("ij,bjk->bik", lower_mask, blocked, preferred_element_type=jnp.float32)
    totals = jnp.sum(blocked.astype(jnp.float32), axis=1)
    block_index = jnp.arange(block_count, dtype=jnp.int32)
    block_lower = (block_index[:, None] > block_index[None, :]).astype(jnp.float32)
    before = jnp.dot(block_lower, totals, precision=HIGHEST)
    running = within + before[:, None, :]
    ranks = jnp.sum(running * blocked.astype(jnp.float32), axis=2)
    return ranks.reshape(total_rows).astype(jnp.int32)


def request_tables(token_ids, counts, lengths, token_rows, device_count, capacity):
    host_count, slot_count = token_ids.shape
    alive_mask = jnp.arange(slot_count, dtype=jnp.int32)[None, :] < lengths[:, None]
    owners = jnp.where(alive_mask, token_ids // token_rows, device_count).reshape(-1)
    local_rows = (token_ids % token_rows).reshape(-1)
    hosts = jnp.arange(host_count, dtype=jnp.int32)[:, None]
    codes = ((hosts + 1) * COUNT_SPAN + counts).reshape(-1)
    total_rows = host_count * slot_count
    block_rows = math.gcd(total_rows, 512)
    block_count = total_rows // block_rows
    owner_hot = (owners[:, None] == jnp.arange(device_count + 1, dtype=jnp.int32)[None, :]).astype(
        jnp.bfloat16
    )
    ranks = owner_ranks(owner_hot, block_rows)
    capacity_index = jnp.arange(capacity, dtype=jnp.int32)

    def place_block(total, packed):
        hot_block, row_block, code_block, rank_block = packed
        hot = hot_block[:, :device_count].astype(jnp.float32)
        valued = jnp.concatenate(
            [
                hot * row_block.astype(jnp.float32)[:, None],
                hot * code_block.astype(jnp.float32)[:, None],
            ],
            axis=1,
        )
        rank_hot = (rank_block[:, None] == capacity_index[None, :]).astype(jnp.float32)
        placed = lax.dot_general(
            valued,
            rank_hot,
            (((0,), (0,)), ((), ())),
            precision=HIGHEST,
            preferred_element_type=jnp.float32,
        )
        return (total + placed, None)

    tables, unused = lax.scan(
        place_block,
        jnp.zeros((2 * device_count, capacity), jnp.float32),
        (
            owner_hot.reshape(block_count, block_rows, device_count + 1),
            local_rows.reshape(block_count, block_rows),
            codes.reshape(block_count, block_rows),
            ranks.reshape(block_count, block_rows),
        ),
    )
    return tables[:device_count], tables[device_count:].astype(jnp.int32)


def split_pair(values):
    high = values.astype(jnp.bfloat16)
    low = (values - high.astype(jnp.float32)).astype(jnp.bfloat16)
    return jnp.concatenate([high, low], axis=0)


def spread(capacity, rows_ref, code_ref, vectors, first, scratch_ref):
    host_count = vectors.shape[0]
    halves = split_pair(vectors)
    scratch_ref[...] = jnp.zeros_like(scratch_ref)
    row_host = lax.broadcasted_iota(jnp.int32, (host_count, capacity), 0) + 1

    @pl.loop(0, rows_ref.shape[0])
    def _(block):
        rows = rows_ref[block, :capacity, :]
        code = code_ref[pl.ds(block, 1), :]
        both = lax.dot_general(
            halves, rows, (((1,), (1,)), ((), ())), preferred_element_type=jnp.float32
        )
        inner = both[:host_count] + both[host_count:]
        weight = CONFIDENCE_SCALE * (code % COUNT_SPAN).astype(jnp.float32)
        if first:
            value = (1.0 + weight) - weight * inner
        else:
            value = weight * inner
        masked = jnp.where(row_host == code // COUNT_SPAN, value, 0.0)
        out = jnp.dot(split_pair(masked), rows, preferred_element_type=jnp.float32)
        scratch_ref[...] += out[:host_count] + out[host_count:]

    return scratch_ref[...]


def solve_body(capacity, rows_ref, code_ref, gram_ref, start_ref, out_ref, scratch_ref):
    def smooth(vectors):
        return (
            jnp.dot(
                vectors, gram_ref[...], precision=HIGHEST, preferred_element_type=jnp.float32
            )
            + RIDGE_WEIGHT * vectors
        )

    iterate = start_ref[...]
    residual = spread(capacity, rows_ref, code_ref, iterate, True, scratch_ref) - smooth(iterate)
    direction = residual
    norm_now = jnp.sum(residual * residual, axis=1, keepdims=True)
    for iteration in range(CG_STEPS):
        image = spread(capacity, rows_ref, code_ref, direction, False, scratch_ref) + smooth(
            direction
        )
        step_size = norm_now / (jnp.sum(direction * image, axis=1, keepdims=True) + SMALL_EPSILON)
        iterate = iterate + step_size * direction
        if iteration < CG_STEPS - 1:
            residual = residual - step_size * image
            norm_next = jnp.sum(residual * residual, axis=1, keepdims=True)
            direction = residual + norm_next / (norm_now + SMALL_EPSILON) * direction
            norm_now = norm_next
    out_ref[...] = iterate


def shards(host_factors, token_ids, counts, lengths, token_factors):
    axes = ("shard", "sub")
    device_count = lax.axis_size(axes)
    token_rows = token_factors.shape[0]
    host_count, slot_count = token_ids.shape
    width = host_factors.shape[1]
    capacity = max(4, host_count * slot_count // device_count)
    share = width // device_count
    partial_gram = lax.dot_general(
        token_factors, token_factors, (((0,), (0,)), ((), ())), preferred_element_type=jnp.float32
    )
    wanted, codes = request_tables(
        token_ids, counts, lengths, token_rows, device_count, capacity
    )
    outgoing = jnp.concatenate([partial_gram.reshape(device_count, share * width), wanted], axis=1)
    incoming = lax.all_to_all(outgoing, axes, split_axis=0, concat_axis=0, tiled=True)
    requests = incoming[:, share * width :].astype(jnp.int32)
    gram_share = jnp.sum(incoming[:, : share * width], axis=0).reshape(share, width)
    high = lax.reduce_precision(gram_share, 8, 7)
    low = gram_share - high
    pair = jnp.concatenate([high, low], axis=0).astype(jnp.bfloat16)
    located = jnp.concatenate(
        [
            token_factors[requests],
            jnp.broadcast_to(pair[None], (device_count, 2 * share, width)),
        ],
        axis=1,
    )
    fetched = lax.all_to_all(located, axes, split_axis=0, concat_axis=0, tiled=True)
    gram_matrix = (
        fetched[:, capacity : capacity + share].astype(jnp.float32)
        + fetched[:, capacity + share :].astype(jnp.float32)
    ).reshape(width, width)
    return pl.pallas_call(
        functools.partial(solve_body, capacity),
        out_shape=jax.ShapeDtypeStruct((host_count, width), jnp.float32),
        in_specs=[pl.BlockSpec(memory_space=pltpu.VMEM)] * 4,
        out_specs=pl.BlockSpec(memory_space=pltpu.VMEM),
        scratch_shapes=[pltpu.VMEM((host_count, width), jnp.float32)],
        compiler_params=pltpu.CompilerParams(vmem_limit_bytes=32 * 1024 * 1024),
    )(fetched, codes, gram_matrix, host_factors)


def solution(mesh):
    placed = (
        P(("parts", "shard", "sub"), None),
        P(("parts", "shard", "sub"), None),
        P(("parts", "shard", "sub"), None),
        P(("parts", "shard", "sub")),
        P(("parts", "shard", "sub"), None),
    )
    return jax.shard_map(
        shards,
        mesh=mesh,
        in_specs=placed,
        out_specs=P(("parts", "shard", "sub"), None),
        check_vma=False,
    )
```

```python
import functools
import math

import jax
import jax.numpy as jnp
from jax import lax
from jax.experimental import pallas as pl
from jax.experimental.pallas import tpu as pltpu
from jax.sharding import PartitionSpec as P

CG_STEPS = 3
CONFIDENCE_SCALE = 40.0
RIDGE_WEIGHT = 0.1
SMALL_EPSILON = 1e-06
HIGHEST = lax.Precision.HIGHEST
COUNT_SPAN = 64


def owner_ranks(owner_hot, block_rows):
    total_rows, owner_width = owner_hot.shape
    block_count = total_rows // block_rows
    blocked = owner_hot.reshape(block_count, block_rows, owner_width)
    position = jnp.arange(block_rows, dtype=jnp.int32)
    lower_mask = (position[:, None] > position[None, :]).astype(jnp.bfloat16)
    within = jnp.einsum("ij,bjk->bik", lower_mask, blocked, preferred_element_type=jnp.float32)
    totals = jnp.sum(blocked.astype(jnp.float32), axis=1)
    block_index = jnp.arange(block_count, dtype=jnp.int32)
    block_lower = (block_index[:, None] > block_index[None, :]).astype(jnp.float32)
    before = jnp.dot(block_lower, totals, precision=HIGHEST)
    running = within + before[:, None, :]
    ranks = jnp.sum(running * blocked.astype(jnp.float32), axis=2)
    return ranks.reshape(total_rows).astype(jnp.int32)


def request_tables(token_ids, counts, lengths, token_rows, device_count, capacity):
    host_count, slot_count = token_ids.shape
    alive_mask = jnp.arange(slot_count, dtype=jnp.int32)[None, :] < lengths[:, None]
    owners = jnp.where(alive_mask, token_ids // token_rows, device_count).reshape(-1)
    local_rows = (token_ids % token_rows).reshape(-1)
    hosts = jnp.arange(host_count, dtype=jnp.int32)[:, None]
    codes = ((hosts + 1) * COUNT_SPAN + counts).reshape(-1)
    total_rows = host_count * slot_count
    block_rows = math.gcd(total_rows, 512)
    block_count = total_rows // block_rows
    owner_hot = (owners[:, None] == jnp.arange(device_count + 1, dtype=jnp.int32)[None, :]).astype(
        jnp.bfloat16
    )
    ranks = owner_ranks(owner_hot, block_rows)
    capacity_index = jnp.arange(capacity, dtype=jnp.int32)

    def place_block(total, packed):
        hot_block, row_block, code_block, rank_block = packed
        hot = hot_block[:, :device_count].astype(jnp.float32)
        valued = jnp.concatenate(
            [
                hot * row_block.astype(jnp.float32)[:, None],
                hot * code_block.astype(jnp.float32)[:, None],
            ],
            axis=1,
        )
        rank_hot = (rank_block[:, None] == capacity_index[None, :]).astype(jnp.float32)
        placed = lax.dot_general(
            valued,
            rank_hot,
            (((0,), (0,)), ((), ())),
            precision=HIGHEST,
            preferred_element_type=jnp.float32,
        )
        return (total + placed, None)

    tables, unused = lax.scan(
        place_block,
        jnp.zeros((2 * device_count, capacity), jnp.float32),
        (
            owner_hot.reshape(block_count, block_rows, device_count + 1),
            local_rows.reshape(block_count, block_rows),
            codes.reshape(block_count, block_rows),
            ranks.reshape(block_count, block_rows),
        ),
    )
    return tables[:device_count], tables[device_count:].astype(jnp.int32)


def split_pair(values):
    high = values.astype(jnp.bfloat16)
    low = (values - high.astype(jnp.float32)).astype(jnp.bfloat16)
    return jnp.concatenate([high, low], axis=0)


def solve_body(
    sizes,
    token_ref,
    wanted_ref,
    code_ref,
    start_ref,
    out_ref,
    token_wide,
    asked,
    asked_scalar,
    staged_wide,
    staged,
    fetched,
    gram_own,
    gram_parts,
    gram_whole,
    total_ref,
    scalar_sem,
    ask_send,
    ask_recv,
    part_send,
    part_recv,
    sum_send,
    sum_recv,
    row_send,
    row_recv,
):
    outer, inner, capacity, group = sizes
    count = outer * inner
    owners, share, width = gram_whole.shape
    at_outer, at_inner = lax.axis_index("shard"), lax.axis_index("sub")
    me = at_outer * inner + at_inner

    def partner(offset):
        there_outer = lax.rem(at_outer + lax.rem(offset, outer), outer)
        there_inner = lax.rem(at_inner + offset // outer, inner)
        return there_outer * inner + there_inner, {"shard": there_outer, "sub": there_inner}

    def each_partner(action):
        @pl.loop(0, count - 1)
        def _(step):
            action(*partner(count - 1 - step))

    def where_owner(device, action):
        if owners == count:
            action()
        else:
            pl.when(device < owners)(action)

    def ask_copy(there, where, slot):
        return pltpu.make_async_remote_copy(
            src_ref=wanted_ref.at[there],
            dst_ref=asked.at[slot],
            send_sem=ask_send.at[there],
            recv_sem=ask_recv.at[slot],
            device_id=where,
            device_id_type=pl.DeviceIdType.MESH,
        )

    def part_copy(there, where, slot):
        return pltpu.make_async_remote_copy(
            src_ref=gram_own.at[there],
            dst_ref=gram_parts.at[slot],
            send_sem=part_send.at[there],
            recv_sem=part_recv.at[slot],
            device_id=where,
            device_id_type=pl.DeviceIdType.MESH,
        )

    def sum_copy(there, where, slot):
        return pltpu.make_async_remote_copy(
            src_ref=gram_whole.at[slot],
            dst_ref=gram_whole.at[slot],
            send_sem=sum_send.at[there],
            recv_sem=sum_recv.at[slot],
            device_id=where,
            device_id_type=pl.DeviceIdType.MESH,
        )

    def row_copy(there, where, slot):
        return pltpu.make_async_remote_copy(
            src_ref=staged.at[there],
            dst_ref=fetched.at[slot],
            send_sem=row_send.at[there],
            recv_sem=row_recv.at[slot],
            device_id=where,
            device_id_type=pl.DeviceIdType.MESH,
        )

    barrier = pltpu.get_barrier_semaphore()
    each_partner(
        lambda there, where: pl.semaphore_signal(
            barrier, inc=1, device_id=where, device_id_type=pl.DeviceIdType.MESH
        )
    )
    pl.semaphore_wait(barrier, count - 1)
    each_partner(lambda there, where: ask_copy(there, where, me).start())

    total_ref[...] = jnp.zeros_like(total_ref)
    strip = math.gcd(token_ref.shape[0], 1024)

    @pl.loop(0, token_ref.shape[0] // strip)
    def _(index):
        at = pl.ds(pl.multiple_of(index * strip, strip), strip)
        rows = token_ref[at, :]
        token_wide[at, :] = rows.astype(jnp.float32)
        total_ref[...] += lax.dot_general(
            rows, rows, (((0,), (0,)), ((), ())), preferred_element_type=jnp.float32
        )

    gram_own[...] = total_ref[...].reshape(owners, share, width)
    each_partner(
        lambda there, where: where_owner(there, lambda: part_copy(there, where, me).start())
    )

    each_partner(lambda there, where: ask_copy(there, where, there).wait_recv())
    asked[pl.ds(me, 1)] = wanted_ref[pl.ds(me, 1)]
    to_scalar = pltpu.make_async_copy(asked, asked_scalar, scalar_sem)
    to_scalar.start()
    to_scalar.wait()

    def collect(there, target):
        burst = math.gcd(capacity, 32)

        @pl.loop(0, capacity // burst)
        def _(index):
            first = pl.multiple_of(index * burst, burst)
            for row in range(burst):
                chosen = asked_scalar[there, 0, first + row]
                staged_wide[pl.ds(first + row, 1), :] = token_wide[pl.ds(chosen, 1), :]

        target[there] = staged_wide[...].astype(jnp.bfloat16)

    def serve(there, where):
        collect(there, staged)
        row_copy(there, where, me).start()

    each_partner(serve)
    collect(me, fetched)

    def reduce_part():
        gram_parts[pl.ds(me, 1)] = gram_own[pl.ds(me, 1)]
        each_partner(lambda there, where: part_copy(me, where, there).wait_recv())
        gram_whole[pl.ds(me, 1)] = jnp.sum(gram_parts[...], axis=0, keepdims=True)
        each_partner(lambda there, where: sum_copy(there, where, me).start())

    where_owner(me, reduce_part)

    host_count = start_ref.shape[0]
    row_host = lax.broadcasted_iota(jnp.int32, (host_count, group * capacity), 0) + 1

    def inner_products(index, halves):
        rows = fetched[pl.ds(index * group, group)].reshape(group * capacity, width)
        both = lax.dot_general(
            halves, rows, (((1,), (1,)), ((), ())), preferred_element_type=jnp.float32
        )
        code = code_ref[index]
        weight = CONFIDENCE_SCALE * (code % COUNT_SPAN).astype(jnp.float32)
        return rows, both[:host_count] + both[host_count:], row_host == code // COUNT_SPAN, weight

    def add_rows(masked, rows):
        out = jnp.dot(split_pair(masked), rows, preferred_element_type=jnp.float32)
        total_ref[...] += out[:host_count] + out[host_count:]

    def spread(vectors, first):
        halves = split_pair(vectors)
        total_ref[...] = jnp.zeros_like(total_ref)

        @pl.loop(0, count // group)
        def _(index):
            rows, product, own, weight = inner_products(index, halves)
            value = (1.0 + weight) - weight * product if first else weight * product
            add_rows(jnp.where(own, value, 0.0), rows)

        return total_ref[...]

    def smooth(vectors):
        gram = gram_whole[...].reshape(width, width)
        return (
            jnp.dot(vectors, gram, precision=HIGHEST, preferred_element_type=jnp.float32)
            + RIDGE_WEIGHT * vectors
        )

    each_partner(lambda there, where: row_copy(there, where, there).wait_recv())
    iterate = start_ref[...]
    residual = spread(iterate, True)
    each_partner(
        lambda there, where: where_owner(there, lambda: sum_copy(there, where, there).wait_recv())
    )
    residual = residual - smooth(iterate)
    direction = residual
    norm_now = jnp.sum(residual * residual, axis=1, keepdims=True)
    for iteration in range(CG_STEPS):
        image = spread(direction, False) + smooth(direction)
        step_size = norm_now / (jnp.sum(direction * image, axis=1, keepdims=True) + SMALL_EPSILON)
        iterate = iterate + step_size * direction
        if iteration < CG_STEPS - 1:
            residual = residual - step_size * image
            norm_next = jnp.sum(residual * residual, axis=1, keepdims=True)
            direction = residual + norm_next / (norm_now + SMALL_EPSILON) * direction
            norm_now = norm_next
    out_ref[...] = iterate

    def settle(there, where):
        ask_copy(there, where, me).wait_send()
        where_owner(there, lambda: part_copy(there, where, me).wait_send())
        where_owner(me, lambda: sum_copy(there, where, me).wait_send())
        row_copy(there, where, me).wait_send()

    each_partner(settle)


def shards(host_factors, token_ids, counts, lengths, token_factors):
    outer, inner = lax.axis_size("shard"), lax.axis_size("sub")
    device_count = outer * inner
    token_rows = token_factors.shape[0]
    host_count, slot_count = token_ids.shape
    width = host_factors.shape[1]
    capacity = max(16, host_count * slot_count // device_count)
    share = max(8, width // device_count)
    owners = width // share
    group = math.gcd(device_count, max(1, 1024 // capacity))
    wanted, codes = request_tables(
        token_ids, counts, lengths, token_rows, device_count, capacity
    )
    wanted = wanted.astype(jnp.int32).reshape(device_count, 1, capacity)
    codes = codes.reshape(device_count // group, 1, group * capacity)
    in_vmem = pl.BlockSpec(memory_space=pltpu.VMEM)
    links = [pltpu.SemaphoreType.DMA((device_count,))] * 8
    return pl.pallas_call(
        functools.partial(solve_body, (outer, inner, capacity, group)),
        out_shape=jax.ShapeDtypeStruct((host_count, width), jnp.float32),
        in_specs=[in_vmem] * 4,
        out_specs=in_vmem,
        scratch_shapes=[
            pltpu.VMEM((token_rows, width), jnp.float32),
            pltpu.VMEM((device_count, 1, capacity), jnp.int32),
            pltpu.SMEM((device_count, 1, capacity), jnp.int32),
            pltpu.VMEM((capacity, width), jnp.float32),
            pltpu.VMEM((device_count, capacity, width), jnp.bfloat16),
            pltpu.VMEM((device_count, capacity, width), jnp.bfloat16),
            pltpu.VMEM((owners, share, width), jnp.float32),
            pltpu.VMEM((device_count, share, width), jnp.float32),
            pltpu.VMEM((owners, share, width), jnp.float32),
            pltpu.VMEM((host_count, width), jnp.float32),
            pltpu.SemaphoreType.DMA,
        ]
        + links,
        compiler_params=pltpu.CompilerParams(
            vmem_limit_bytes=48 * 1024 * 1024, collective_id=0, has_side_effects=True
        ),
    )(token_factors, wanted, codes, host_factors)


def solution(mesh):
    placed = (
        P(("parts", "shard", "sub"), None),
        P(("parts", "shard", "sub"), None),
        P(("parts", "shard", "sub"), None),
        P(("parts", "shard", "sub")),
        P(("parts", "shard", "sub"), None),
    )
    return jax.shard_map(
        shards,
        mesh=mesh,
        in_specs=placed,
        out_specs=P(("parts", "shard", "sub"), None),
        check_vma=False,
    )
```

```python
import functools
import math

import jax
import jax.numpy as jnp
from jax import lax
from jax.experimental import pallas as pl
from jax.experimental.pallas import tpu as pltpu
from jax.sharding import PartitionSpec as P

CG_STEPS = 3
CONFIDENCE_SCALE = 40.0
RIDGE_WEIGHT = 0.1
SMALL_EPSILON = 1e-06
HIGHEST = lax.Precision.HIGHEST
COUNT_SPAN = 64
DIGIT = 128


def owner_ranks(owner_hot, block_rows):
    total_rows, owner_width = owner_hot.shape
    block_count = total_rows // block_rows
    blocked = owner_hot.reshape(block_count, block_rows, owner_width)
    position = jnp.arange(block_rows, dtype=jnp.int32)
    lower_mask = (position[:, None] > position[None, :]).astype(jnp.bfloat16)
    within = jnp.einsum("ij,bjk->bik", lower_mask, blocked, preferred_element_type=jnp.float32)
    totals = jnp.sum(blocked.astype(jnp.float32), axis=1)
    block_index = jnp.arange(block_count, dtype=jnp.int32)
    block_lower = (block_index[:, None] > block_index[None, :]).astype(jnp.float32)
    before = jnp.dot(block_lower, totals, precision=HIGHEST)
    running = within + before[:, None, :]
    ranks = jnp.sum(running * blocked.astype(jnp.float32), axis=2)
    return ranks.reshape(total_rows).astype(jnp.int32)


def request_tables(token_ids, counts, lengths, token_rows, device_count, capacity):
    host_count, slot_count = token_ids.shape
    alive_mask = jnp.arange(slot_count, dtype=jnp.int32)[None, :] < lengths[:, None]
    owners = jnp.where(alive_mask, token_ids // token_rows, device_count).reshape(-1)
    local_rows = (token_ids % token_rows).reshape(-1)
    hosts = jnp.arange(host_count, dtype=jnp.int32)[:, None]
    codes = ((hosts + 1) * COUNT_SPAN + counts).reshape(-1)
    total_rows = host_count * slot_count
    block_rows = math.gcd(total_rows, 512)
    owner_hot = (owners[:, None] == jnp.arange(device_count + 1, dtype=jnp.int32)[None, :]).astype(
        jnp.bfloat16
    )
    ranks = owner_ranks(owner_hot, block_rows)
    capacity_index = jnp.arange(capacity, dtype=jnp.int32)

    digits = jnp.stack(
        [local_rows // DIGIT, local_rows % DIGIT, codes // DIGIT, codes % DIGIT], axis=1
    ).astype(jnp.bfloat16)
    valued = (digits[:, :, None] * owner_hot[:, None, :device_count]).reshape(
        total_rows, 4 * device_count
    )
    rank_hot = (ranks[:, None] == capacity_index[None, :]).astype(jnp.bfloat16)
    placed = lax.dot_general(
        valued, rank_hot, (((0,), (0,)), ((), ())), preferred_element_type=jnp.float32
    )
    placed = placed.astype(jnp.int32).reshape(4, device_count, capacity)
    return placed[0] * DIGIT + placed[1], placed[2] * DIGIT + placed[3]


def split_pair(values):
    high = values.astype(jnp.bfloat16)
    low = (values - high.astype(jnp.float32)).astype(jnp.bfloat16)
    return jnp.concatenate([high, low], axis=0)


def solve_body(
    sizes,
    token_ref,
    wanted_ref,
    code_ref,
    start_ref,
    out_ref,
    token_wide,
    asked,
    asked_scalar,
    staged_wide,
    staged,
    fetched,
    gram_own,
    gram_parts,
    gram_whole,
    total_ref,
    scalar_sem,
    ask_send,
    ask_recv,
    part_send,
    part_recv,
    sum_send,
    sum_recv,
    row_send,
    row_recv,
):
    outer, inner, capacity = sizes
    group = outer
    count = outer * inner
    owners, share, width = gram_whole.shape
    at_outer, at_inner = lax.axis_index("shard"), lax.axis_index("sub")
    me = at_outer * inner + at_inner
    my_place = at_inner * outer + at_outer

    def partner(offset):
        there_outer = lax.rem(at_outer + lax.rem(offset, outer), outer)
        there_inner = lax.rem(at_inner + offset // outer, inner)
        return there_outer * inner + there_inner, {"shard": there_outer, "sub": there_inner}

    def each_partner(action, first=0, last=count - 1):
        @pl.loop(first, last)
        def _(step):
            action(*partner(count - 1 - step))

    def where_owner(device, action):
        if owners == count:
            action()
        else:
            pl.when(device < owners)(action)

    def ask_copy(there, where, slot):
        return pltpu.make_async_remote_copy(
            src_ref=wanted_ref.at[there],
            dst_ref=asked.at[slot],
            send_sem=ask_send.at[there],
            recv_sem=ask_recv.at[slot],
            device_id=where,
            device_id_type=pl.DeviceIdType.MESH,
        )

    def part_copy(there, where, slot):
        return pltpu.make_async_remote_copy(
            src_ref=gram_own.at[there],
            dst_ref=gram_parts.at[slot],
            send_sem=part_send.at[there],
            recv_sem=part_recv.at[slot],
            device_id=where,
            device_id_type=pl.DeviceIdType.MESH,
        )

    def sum_copy(there, where, slot):
        return pltpu.make_async_remote_copy(
            src_ref=gram_whole.at[slot],
            dst_ref=gram_whole.at[slot],
            send_sem=sum_send.at[there],
            recv_sem=sum_recv.at[slot],
            device_id=where,
            device_id_type=pl.DeviceIdType.MESH,
        )

    def row_copy(there, where, slot):
        return pltpu.make_async_remote_copy(
            src_ref=staged.at[there],
            dst_ref=fetched.at[slot],
            send_sem=row_send.at[there],
            recv_sem=row_recv.at[slot],
            device_id=where,
            device_id_type=pl.DeviceIdType.MESH,
        )

    barrier = pltpu.get_barrier_semaphore()
    each_partner(
        lambda there, where: pl.semaphore_signal(
            barrier, inc=1, device_id=where, device_id_type=pl.DeviceIdType.MESH
        )
    )
    pl.semaphore_wait(barrier, count - 1)
    each_partner(lambda there, where: ask_copy(there, where, me).start())

    strip = math.gcd(token_ref.shape[0], 1024)

    @pl.loop(0, token_ref.shape[0] // strip)
    def _(index):
        at = pl.ds(pl.multiple_of(index * strip, strip), strip)
        token_wide[at, :] = token_ref[at, :].astype(jnp.float32)

    each_partner(lambda there, where: ask_copy(there, where, there).wait_recv())
    asked[pl.ds(me, 1)] = wanted_ref[pl.ds(me, 1)]
    to_scalar = pltpu.make_async_copy(asked, asked_scalar, scalar_sem)
    to_scalar.start()
    to_scalar.wait()

    def collect(there, target, place):
        burst = math.gcd(capacity, 32)

        @pl.loop(0, capacity // burst)
        def _(index):
            first = pl.multiple_of(index * burst, burst)
            for row in range(burst):
                chosen = asked_scalar[there, 0, first + row]
                staged_wide[pl.ds(first + row, 1), :] = token_wide[pl.ds(chosen, 1), :]

        target[place] = staged_wide[...].astype(jnp.bfloat16)

    def serve(there, where):
        collect(there, staged, there)
        row_copy(there, where, my_place).start()

    half = count // 2
    each_partner(serve, 0, half)

    total_ref[...] = jnp.zeros_like(total_ref)

    @pl.loop(0, token_ref.shape[0] // strip)
    def _(index):
        rows = token_ref[pl.ds(pl.multiple_of(index * strip, strip), strip), :]
        total_ref[...] += lax.dot_general(
            rows, rows, (((0,), (0,)), ((), ())), preferred_element_type=jnp.float32
        )

    gram_own[...] = total_ref[...].reshape(owners, share, width)
    each_partner(
        lambda there, where: where_owner(there, lambda: part_copy(there, where, me).start())
    )
    each_partner(serve, half, count - 1)
    collect(me, fetched, my_place)

    def reduce_part():
        gram_parts[pl.ds(me, 1)] = gram_own[pl.ds(me, 1)]
        each_partner(lambda there, where: part_copy(me, where, there).wait_recv())
        gram_whole[pl.ds(me, 1)] = jnp.sum(gram_parts[...], axis=0, keepdims=True)
        each_partner(lambda there, where: sum_copy(there, where, me).start())

    where_owner(me, reduce_part)

    host_count = start_ref.shape[0]
    row_host = lax.broadcasted_iota(jnp.int32, (host_count, group * capacity), 0) + 1

    def inner_products(index, halves):
        rows = fetched[pl.ds(index * group, group)].reshape(group * capacity, width)
        both = lax.dot_general(
            halves, rows, (((1,), (1,)), ((), ())), preferred_element_type=jnp.float32
        )
        code = code_ref[index]
        weight = CONFIDENCE_SCALE * (code % COUNT_SPAN).astype(jnp.float32)
        return rows, both[:host_count] + both[host_count:], row_host == code // COUNT_SPAN, weight

    def add_rows(masked, rows):
        out = jnp.dot(split_pair(masked), rows, preferred_element_type=jnp.float32)
        total_ref[...] += out[:host_count] + out[host_count:]

    def first_spread(vectors):
        halves = split_pair(vectors)
        total_ref[...] = jnp.zeros_like(total_ref)

        def arrive(index, source):
            where = {"shard": source, "sub": index}
            row_copy(source * inner + index, where, index * outer + source).wait_recv()

        def add_group(index):
            rows, product, own, weight = inner_products(index, halves)
            add_rows(jnp.where(own, (1.0 + weight) - weight * product, 0.0), rows)

        @pl.loop(0, inner - 1)
        def _(step):
            index = lax.rem(at_inner + 1 + step, inner)

            @pl.loop(0, outer)
            def _(source):
                arrive(index, source)

            add_group(index)

        @pl.loop(0, outer - 1)
        def _(step):
            arrive(at_inner, lax.rem(at_outer + 1 + step, outer))

        add_group(at_inner)
        return total_ref[...]

    def spread(vectors):
        halves = split_pair(vectors)
        total_ref[...] = jnp.zeros_like(total_ref)

        @pl.loop(0, inner)
        def _(index):
            rows, product, own, weight = inner_products(index, halves)
            add_rows(jnp.where(own, weight * product, 0.0), rows)

        return total_ref[...]

    def squares(vectors):
        halves = split_pair(vectors)

        def add(index, total):
            rows, product, own, weight = inner_products(index, halves)
            value = jnp.where(own, weight * product * product, 0.0)
            return total + jnp.sum(value, axis=1, keepdims=True)

        return lax.fori_loop(0, inner, add, jnp.zeros((host_count, 1), jnp.float32))

    def smooth(vectors):
        gram = gram_whole[...].reshape(width, width)
        return (
            jnp.dot(vectors, gram, precision=HIGHEST, preferred_element_type=jnp.float32)
            + RIDGE_WEIGHT * vectors
        )

    iterate = start_ref[...]
    residual = first_spread(iterate)
    each_partner(
        lambda there, where: where_owner(there, lambda: sum_copy(there, where, there).wait_recv())
    )
    residual = residual - smooth(iterate)
    direction = residual
    norm_now = jnp.sum(residual * residual, axis=1, keepdims=True)
    for iteration in range(CG_STEPS):
        image = smooth(direction)
        if iteration < CG_STEPS - 1:
            image = image + spread(direction)
            along = jnp.sum(direction * image, axis=1, keepdims=True)
        else:
            along = jnp.sum(direction * image, axis=1, keepdims=True) + squares(direction)
        step_size = norm_now / (along + SMALL_EPSILON)
        iterate = iterate + step_size * direction
        if iteration < CG_STEPS - 1:
            residual = residual - step_size * image
            norm_next = jnp.sum(residual * residual, axis=1, keepdims=True)
            direction = residual + norm_next / (norm_now + SMALL_EPSILON) * direction
            norm_now = norm_next
    out_ref[...] = iterate

    def settle(there, where):
        ask_copy(there, where, me).wait_send()
        where_owner(there, lambda: part_copy(there, where, me).wait_send())
        where_owner(me, lambda: sum_copy(there, where, me).wait_send())
        row_copy(there, where, my_place).wait_send()

    each_partner(settle)


def shards(host_factors, token_ids, counts, lengths, token_factors):
    outer, inner = lax.axis_size("shard"), lax.axis_size("sub")
    device_count = outer * inner
    token_rows = token_factors.shape[0]
    host_count, slot_count = token_ids.shape
    width = host_factors.shape[1]
    capacity = max(16, host_count * slot_count // device_count)
    share = max(8, width // device_count)
    owners = width // share
    wanted, codes = request_tables(
        token_ids, counts, lengths, token_rows, device_count, capacity
    )
    wanted = wanted.reshape(device_count, 1, capacity)
    codes = codes.reshape(outer, inner, capacity).transpose(1, 0, 2)
    codes = codes.reshape(inner, 1, outer * capacity)
    in_vmem = pl.BlockSpec(memory_space=pltpu.VMEM)
    links = [pltpu.SemaphoreType.DMA((device_count,))] * 8
    return pl.pallas_call(
        functools.partial(solve_body, (outer, inner, capacity)),
        out_shape=jax.ShapeDtypeStruct((host_count, width), jnp.float32),
        in_specs=[in_vmem] * 4,
        out_specs=in_vmem,
        scratch_shapes=[
            pltpu.VMEM((token_rows, width), jnp.float32),
            pltpu.VMEM((device_count, 1, capacity), jnp.int32),
            pltpu.SMEM((device_count, 1, capacity), jnp.int32),
            pltpu.VMEM((capacity, width), jnp.float32),
            pltpu.VMEM((device_count, capacity, width), jnp.bfloat16),
            pltpu.VMEM((device_count, capacity, width), jnp.bfloat16),
            pltpu.VMEM((owners, share, width), jnp.float32),
            pltpu.VMEM((device_count, share, width), jnp.float32),
            pltpu.VMEM((owners, share, width), jnp.float32),
            pltpu.VMEM((host_count, width), jnp.float32),
            pltpu.SemaphoreType.DMA,
        ]
        + links,
        compiler_params=pltpu.CompilerParams(
            vmem_limit_bytes=48 * 1024 * 1024, collective_id=0, has_side_effects=True
        ),
    )(token_factors, wanted, codes, host_factors)


def solution(mesh):
    placed = (
        P(("parts", "shard", "sub"), None),
        P(("parts", "shard", "sub"), None),
        P(("parts", "shard", "sub"), None),
        P(("parts", "shard", "sub")),
        P(("parts", "shard", "sub"), None),
    )
    return jax.shard_map(
        shards,
        mesh=mesh,
        in_specs=placed,
        out_specs=P(("parts", "shard", "sub"), None),
        check_vma=False,
    )
```

```python
import functools
import math

import jax
import jax.numpy as jnp
from jax import lax
from jax.experimental import pallas as pl
from jax.experimental.pallas import tpu as pltpu
from jax.sharding import PartitionSpec as P

CG_STEPS = 3
CONFIDENCE_SCALE = 40.0
RIDGE_WEIGHT = 0.1
SMALL_EPSILON = 1e-06
HIGHEST = lax.Precision.HIGHEST
COUNT_SPAN = 64
DIGIT = 128


def owner_ranks(owner_hot, block_rows):
    total_rows, owner_width = owner_hot.shape
    block_count = total_rows // block_rows
    blocked = owner_hot.reshape(block_count, block_rows, owner_width)
    position = jnp.arange(block_rows, dtype=jnp.int32)
    lower_mask = (position[:, None] > position[None, :]).astype(jnp.bfloat16)
    within = jnp.einsum("ij,bjk->bik", lower_mask, blocked, preferred_element_type=jnp.float32)
    totals = jnp.sum(blocked.astype(jnp.float32), axis=1)
    block_index = jnp.arange(block_count, dtype=jnp.int32)
    block_lower = (block_index[:, None] > block_index[None, :]).astype(jnp.float32)
    before = jnp.dot(block_lower, totals, precision=HIGHEST)
    running = within + before[:, None, :]
    ranks = jnp.sum(running * blocked.astype(jnp.float32), axis=2)
    return ranks.reshape(total_rows).astype(jnp.int32)


def request_tables(token_ids, counts, lengths, token_rows, device_count, capacity):
    host_count, slot_count = token_ids.shape
    alive_mask = jnp.arange(slot_count, dtype=jnp.int32)[None, :] < lengths[:, None]
    owners = jnp.where(alive_mask, token_ids // token_rows, device_count).reshape(-1)
    local_rows = (token_ids % token_rows).reshape(-1)
    hosts = jnp.arange(host_count, dtype=jnp.int32)[:, None]
    codes = ((hosts + 1) * COUNT_SPAN + counts).reshape(-1)
    total_rows = host_count * slot_count
    block_rows = math.gcd(total_rows, 512)
    owner_hot = (owners[:, None] == jnp.arange(device_count + 1, dtype=jnp.int32)[None, :]).astype(
        jnp.bfloat16
    )
    ranks = owner_ranks(owner_hot, block_rows)
    capacity_index = jnp.arange(capacity, dtype=jnp.int32)

    digits = jnp.stack(
        [local_rows // DIGIT, local_rows % DIGIT, codes // DIGIT, codes % DIGIT], axis=1
    ).astype(jnp.bfloat16)
    valued = (digits[:, :, None] * owner_hot[:, None, :device_count]).reshape(
        total_rows, 4 * device_count
    )
    rank_hot = (ranks[:, None] == capacity_index[None, :]).astype(jnp.bfloat16)
    placed = lax.dot_general(
        valued, rank_hot, (((0,), (0,)), ((), ())), preferred_element_type=jnp.float32
    )
    placed = placed.astype(jnp.int32).reshape(4, device_count, capacity)
    return placed[0] * DIGIT + placed[1], placed[2] * DIGIT + placed[3]


def split_pair(values):
    high = values.astype(jnp.bfloat16)
    low = (values - high.astype(jnp.float32)).astype(jnp.bfloat16)
    return jnp.concatenate([high, low], axis=0)


def solve_body(
    sizes,
    token_ref,
    wanted_ref,
    code_ref,
    start_ref,
    out_ref,
    token_wide,
    asked,
    asked_scalar,
    staged_wide,
    staged,
    fetched,
    gram_own,
    gram_parts,
    gram_whole,
    total_ref,
    scalar_sem,
    ask_send,
    ask_recv,
    part_send,
    part_recv,
    sum_send,
    sum_recv,
    row_send,
    row_recv,
):
    outer, inner, capacity = sizes
    group = outer
    count = outer * inner
    owners, share, width = gram_whole.shape
    at_outer, at_inner = lax.axis_index("shard"), lax.axis_index("sub")
    me = at_outer * inner + at_inner
    my_place = at_inner * outer + at_outer

    def partner(offset):
        there_outer = lax.rem(at_outer + lax.rem(offset, outer), outer)
        there_inner = lax.rem(at_inner + offset // outer, inner)
        return there_outer * inner + there_inner, {"shard": there_outer, "sub": there_inner}

    def each_partner(action):
        @pl.loop(0, count - 1)
        def _(step):
            action(*partner(count - 1 - step))

    def where_owner(device, action):
        if owners == count:
            action()
        else:
            pl.when(device < owners)(action)

    def ask_copy(there, where, slot):
        return pltpu.make_async_remote_copy(
            src_ref=wanted_ref.at[there],
            dst_ref=asked.at[slot],
            send_sem=ask_send.at[there],
            recv_sem=ask_recv.at[slot],
            device_id=where,
            device_id_type=pl.DeviceIdType.MESH,
        )

    def part_copy(there, where, slot):
        return pltpu.make_async_remote_copy(
            src_ref=gram_own.at[there],
            dst_ref=gram_parts.at[slot],
            send_sem=part_send.at[there],
            recv_sem=part_recv.at[slot],
            device_id=where,
            device_id_type=pl.DeviceIdType.MESH,
        )

    def sum_copy(there, where, slot):
        return pltpu.make_async_remote_copy(
            src_ref=gram_whole.at[slot],
            dst_ref=gram_whole.at[slot],
            send_sem=sum_send.at[there],
            recv_sem=sum_recv.at[slot],
            device_id=where,
            device_id_type=pl.DeviceIdType.MESH,
        )

    def row_copy(there, where, slot):
        return pltpu.make_async_remote_copy(
            src_ref=staged.at[there],
            dst_ref=fetched.at[slot],
            send_sem=row_send.at[there],
            recv_sem=row_recv.at[slot],
            device_id=where,
            device_id_type=pl.DeviceIdType.MESH,
        )

    barrier = pltpu.get_barrier_semaphore()
    each_partner(
        lambda there, where: pl.semaphore_signal(
            barrier, inc=1, device_id=where, device_id_type=pl.DeviceIdType.MESH
        )
    )
    pl.semaphore_wait(barrier, count - 1)
    each_partner(lambda there, where: ask_copy(there, where, me).start())

    total_ref[...] = jnp.zeros_like(total_ref)
    strip = math.gcd(token_ref.shape[0], 2048)

    @pl.loop(0, token_ref.shape[0] // strip)
    def _(index):
        at = pl.ds(pl.multiple_of(index * strip, strip), strip)
        rows = token_ref[at, :]
        token_wide[at, :] = rows.astype(jnp.float32)
        total_ref[...] += lax.dot_general(
            rows, rows, (((0,), (0,)), ((), ())), preferred_element_type=jnp.float32
        )

    gram_own[...] = total_ref[...].reshape(owners, share, width)
    each_partner(
        lambda there, where: where_owner(there, lambda: part_copy(there, where, me).start())
    )

    each_partner(lambda there, where: ask_copy(there, where, there).wait_recv())
    asked[pl.ds(me, 1)] = wanted_ref[pl.ds(me, 1)]
    to_scalar = pltpu.make_async_copy(asked, asked_scalar, scalar_sem)
    to_scalar.start()
    to_scalar.wait()

    def collect(there, target, place):
        burst = math.gcd(capacity, 32)

        @pl.loop(0, capacity // burst)
        def _(index):
            first = pl.multiple_of(index * burst, burst)
            for row in range(burst):
                chosen = asked_scalar[there, 0, first + row]
                staged_wide[pl.ds(first + row, 1), :] = token_wide[pl.ds(chosen, 1), :]

        target[place] = staged_wide[...].astype(jnp.bfloat16)

    def serve(there, where):
        collect(there, staged, there)
        row_copy(there, where, my_place).start()

    each_partner(serve)
    collect(me, fetched, my_place)

    def reduce_part():
        gram_parts[pl.ds(me, 1)] = gram_own[pl.ds(me, 1)]
        each_partner(lambda there, where: part_copy(me, where, there).wait_recv())
        gram_whole[pl.ds(me, 1)] = jnp.sum(gram_parts[...], axis=0, keepdims=True)
        each_partner(lambda there, where: sum_copy(there, where, me).start())

    where_owner(me, reduce_part)

    host_count = start_ref.shape[0]
    row_host = lax.broadcasted_iota(jnp.int32, (host_count, group * capacity), 0) + 1

    def inner_products(index, halves):
        rows = fetched[pl.ds(index * group, group)].reshape(group * capacity, width)
        both = lax.dot_general(
            halves, rows, (((1,), (1,)), ((), ())), preferred_element_type=jnp.float32
        )
        code = code_ref[index]
        weight = CONFIDENCE_SCALE * (code % COUNT_SPAN).astype(jnp.float32)
        return rows, both[:host_count] + both[host_count:], row_host == code // COUNT_SPAN, weight

    def add_rows(masked, rows):
        out = jnp.dot(split_pair(masked), rows, preferred_element_type=jnp.float32)
        total_ref[...] += out[:host_count] + out[host_count:]

    def first_spread(vectors):
        halves = split_pair(vectors)
        total_ref[...] = jnp.zeros_like(total_ref)

        def arrive(index, source):
            where = {"shard": source, "sub": index}
            row_copy(source * inner + index, where, index * outer + source).wait_recv()

        def add_group(index):
            rows, product, own, weight = inner_products(index, halves)
            add_rows(jnp.where(own, (1.0 + weight) - weight * product, 0.0), rows)

        @pl.loop(0, inner - 1)
        def _(step):
            index = lax.rem(at_inner + 1 + step, inner)

            @pl.loop(0, outer)
            def _(source):
                arrive(index, source)

            add_group(index)

        @pl.loop(0, outer - 1)
        def _(step):
            arrive(at_inner, lax.rem(at_outer + 1 + step, outer))

        add_group(at_inner)
        return total_ref[...]

    def spread(vectors):
        halves = split_pair(vectors)
        total_ref[...] = jnp.zeros_like(total_ref)

        @pl.loop(0, inner)
        def _(index):
            rows, product, own, weight = inner_products(index, halves)
            add_rows(jnp.where(own, weight * product, 0.0), rows)

        return total_ref[...]

    def squares(vectors):
        halves = split_pair(vectors)

        def add(index, total):
            rows, product, own, weight = inner_products(index, halves)
            value = jnp.where(own, weight * product * product, 0.0)
            return total + jnp.sum(value, axis=1, keepdims=True)

        return lax.fori_loop(0, inner, add, jnp.zeros((host_count, 1), jnp.float32))

    def smooth(vectors):
        gram = gram_whole[...].reshape(width, width)
        return (
            jnp.dot(vectors, gram, precision=HIGHEST, preferred_element_type=jnp.float32)
            + RIDGE_WEIGHT * vectors
        )

    iterate = start_ref[...]
    residual = first_spread(iterate)
    each_partner(
        lambda there, where: where_owner(there, lambda: sum_copy(there, where, there).wait_recv())
    )
    residual = residual - smooth(iterate)
    direction = residual
    norm_now = jnp.sum(residual * residual, axis=1, keepdims=True)
    for iteration in range(CG_STEPS):
        image = smooth(direction)
        if iteration < CG_STEPS - 1:
            image = image + spread(direction)
            along = jnp.sum(direction * image, axis=1, keepdims=True)
        else:
            along = jnp.sum(direction * image, axis=1, keepdims=True) + squares(direction)
        step_size = norm_now / (along + SMALL_EPSILON)
        iterate = iterate + step_size * direction
        if iteration < CG_STEPS - 1:
            residual = residual - step_size * image
            norm_next = jnp.sum(residual * residual, axis=1, keepdims=True)
            direction = residual + norm_next / (norm_now + SMALL_EPSILON) * direction
            norm_now = norm_next
    out_ref[...] = iterate

    def settle(there, where):
        ask_copy(there, where, me).wait_send()
        where_owner(there, lambda: part_copy(there, where, me).wait_send())
        where_owner(me, lambda: sum_copy(there, where, me).wait_send())
        row_copy(there, where, my_place).wait_send()

    each_partner(settle)


def shards(host_factors, token_ids, counts, lengths, token_factors):
    outer, inner = lax.axis_size("shard"), lax.axis_size("sub")
    device_count = outer * inner
    token_rows = token_factors.shape[0]
    host_count, slot_count = token_ids.shape
    width = host_factors.shape[1]
    capacity = max(16, host_count * slot_count // device_count)
    share = max(8, width // device_count)
    owners = width // share
    wanted, codes = request_tables(
        token_ids, counts, lengths, token_rows, device_count, capacity
    )
    wanted = wanted.reshape(device_count, 1, capacity)
    codes = codes.reshape(outer, inner, capacity).transpose(1, 0, 2)
    codes = codes.reshape(inner, 1, outer * capacity)
    in_vmem = pl.BlockSpec(memory_space=pltpu.VMEM)
    links = [pltpu.SemaphoreType.DMA((device_count,))] * 8
    return pl.pallas_call(
        functools.partial(solve_body, (outer, inner, capacity)),
        out_shape=jax.ShapeDtypeStruct((host_count, width), jnp.float32),
        in_specs=[in_vmem] * 4,
        out_specs=in_vmem,
        scratch_shapes=[
            pltpu.VMEM((token_rows, width), jnp.float32),
            pltpu.VMEM((device_count, 1, capacity), jnp.int32),
            pltpu.SMEM((device_count, 1, capacity), jnp.int32),
            pltpu.VMEM((capacity, width), jnp.float32),
            pltpu.VMEM((device_count, capacity, width), jnp.bfloat16),
            pltpu.VMEM((device_count, capacity, width), jnp.bfloat16),
            pltpu.VMEM((owners, share, width), jnp.float32),
            pltpu.VMEM((device_count, share, width), jnp.float32),
            pltpu.VMEM((owners, share, width), jnp.float32),
            pltpu.VMEM((host_count, width), jnp.float32),
            pltpu.SemaphoreType.DMA,
        ]
        + links,
        compiler_params=pltpu.CompilerParams(
            vmem_limit_bytes=48 * 1024 * 1024, collective_id=0, has_side_effects=True
        ),
    )(token_factors, wanted, codes, host_factors)


def solution(mesh):
    placed = (
        P(("parts", "shard", "sub"), None),
        P(("parts", "shard", "sub"), None),
        P(("parts", "shard", "sub"), None),
        P(("parts", "shard", "sub")),
        P(("parts", "shard", "sub"), None),
    )
    return jax.shard_map(
        shards,
        mesh=mesh,
        in_specs=placed,
        out_specs=P(("parts", "shard", "sub"), None),
        check_vma=False,
    )
```

```python
import functools
import math

import jax
import jax.numpy as jnp
from jax import lax
from jax.experimental import pallas as pl
from jax.experimental.pallas import tpu as pltpu
from jax.sharding import PartitionSpec as P

CG_STEPS = 3
CONFIDENCE_SCALE = 40.0
RIDGE_WEIGHT = 0.1
SMALL_EPSILON = 1e-06
HIGHEST = lax.Precision.HIGHEST
COUNT_SPAN = 64
DIGIT = 128


def owner_ranks(owner_hot, block_rows):
    total_rows, owner_width = owner_hot.shape
    block_count = total_rows // block_rows
    blocked = owner_hot.reshape(block_count, block_rows, owner_width)
    position = jnp.arange(block_rows, dtype=jnp.int32)
    lower_mask = (position[:, None] > position[None, :]).astype(jnp.bfloat16)
    within = jnp.einsum("ij,bjk->bik", lower_mask, blocked, preferred_element_type=jnp.float32)
    totals = jnp.sum(blocked.astype(jnp.float32), axis=1)
    block_index = jnp.arange(block_count, dtype=jnp.int32)
    block_lower = (block_index[:, None] > block_index[None, :]).astype(jnp.float32)
    before = jnp.dot(block_lower, totals, precision=HIGHEST)
    running = within + before[:, None, :]
    ranks = jnp.sum(running * blocked.astype(jnp.float32), axis=2)
    return ranks.reshape(total_rows).astype(jnp.int32)


def request_tables(token_ids, counts, lengths, token_rows, device_count, capacity):
    host_count, slot_count = token_ids.shape
    alive_mask = jnp.arange(slot_count, dtype=jnp.int32)[None, :] < lengths[:, None]
    owners = jnp.where(alive_mask, token_ids // token_rows, device_count).reshape(-1)
    local_rows = (token_ids % token_rows).reshape(-1)
    hosts = jnp.arange(host_count, dtype=jnp.int32)[:, None]
    codes = ((hosts + 1) * COUNT_SPAN + counts).reshape(-1)
    total_rows = host_count * slot_count
    block_rows = math.gcd(total_rows, 512)
    owner_hot = (owners[:, None] == jnp.arange(device_count + 1, dtype=jnp.int32)[None, :]).astype(
        jnp.bfloat16
    )
    ranks = owner_ranks(owner_hot, block_rows)
    capacity_index = jnp.arange(capacity, dtype=jnp.int32)

    digits = jnp.stack(
        [local_rows // DIGIT, local_rows % DIGIT, codes // DIGIT, codes % DIGIT], axis=1
    ).astype(jnp.bfloat16)
    valued = (digits[:, :, None] * owner_hot[:, None, :device_count]).reshape(
        total_rows, 4 * device_count
    )
    rank_hot = (ranks[:, None] == capacity_index[None, :]).astype(jnp.bfloat16)
    placed = lax.dot_general(
        valued, rank_hot, (((0,), (0,)), ((), ())), preferred_element_type=jnp.float32
    )
    placed = placed.astype(jnp.int32).reshape(4, device_count, capacity)
    return placed[0] * DIGIT + placed[1], placed[2] * DIGIT + placed[3]


def split_pair(values):
    high = values.astype(jnp.bfloat16)
    low = (values - high.astype(jnp.float32)).astype(jnp.bfloat16)
    return jnp.concatenate([high, low], axis=0)


def solve_body(
    sizes,
    token_home,
    wanted_ref,
    code_ref,
    start_ref,
    out_ref,
    token_ref,
    token_wide,
    asked,
    asked_scalar,
    staged_wide,
    staged,
    fetched,
    gram_own,
    gram_parts,
    gram_whole,
    total_ref,
    scalar_sem,
    token_sem,
    ask_send,
    ask_recv,
    part_send,
    part_recv,
    sum_send,
    sum_recv,
    row_send,
    row_recv,
):
    outer, inner, capacity = sizes
    group = outer
    count = outer * inner
    owners, share, width = gram_whole.shape
    at_outer, at_inner = lax.axis_index("shard"), lax.axis_index("sub")
    me = at_outer * inner + at_inner
    my_place = at_inner * outer + at_outer

    def partner(offset):
        there_outer = lax.rem(at_outer + lax.rem(offset, outer), outer)
        there_inner = lax.rem(at_inner + offset // outer, inner)
        return there_outer * inner + there_inner, {"shard": there_outer, "sub": there_inner}

    def each_partner(action):
        @pl.loop(0, count - 1)
        def _(step):
            action(*partner(count - 1 - step))

    def where_owner(device, action):
        if owners == count:
            action()
        else:
            pl.when(device < owners)(action)

    def ask_copy(there, where, slot):
        return pltpu.make_async_remote_copy(
            src_ref=wanted_ref.at[there],
            dst_ref=asked.at[slot],
            send_sem=ask_send.at[there],
            recv_sem=ask_recv.at[slot],
            device_id=where,
            device_id_type=pl.DeviceIdType.MESH,
        )

    def part_copy(there, where, slot):
        return pltpu.make_async_remote_copy(
            src_ref=gram_own.at[there],
            dst_ref=gram_parts.at[slot],
            send_sem=part_send.at[there],
            recv_sem=part_recv.at[slot],
            device_id=where,
            device_id_type=pl.DeviceIdType.MESH,
        )

    def sum_copy(there, where, slot):
        return pltpu.make_async_remote_copy(
            src_ref=gram_whole.at[slot],
            dst_ref=gram_whole.at[slot],
            send_sem=sum_send.at[there],
            recv_sem=sum_recv.at[slot],
            device_id=where,
            device_id_type=pl.DeviceIdType.MESH,
        )

    def row_copy(there, where, slot):
        return pltpu.make_async_remote_copy(
            src_ref=staged.at[there],
            dst_ref=fetched.at[slot],
            send_sem=row_send.at[there],
            recv_sem=row_recv.at[slot],
            device_id=where,
            device_id_type=pl.DeviceIdType.MESH,
        )

    bring = pltpu.make_async_copy(token_home, token_ref, token_sem)
    bring.start()
    barrier = pltpu.get_barrier_semaphore()
    each_partner(
        lambda there, where: pl.semaphore_signal(
            barrier, inc=1, device_id=where, device_id_type=pl.DeviceIdType.MESH
        )
    )
    pl.semaphore_wait(barrier, count - 1)
    each_partner(lambda there, where: ask_copy(there, where, me).start())

    total_ref[...] = jnp.zeros_like(total_ref)
    bring.wait()
    strip = math.gcd(token_ref.shape[0], 2048)

    @pl.loop(0, token_ref.shape[0] // strip)
    def _(index):
        at = pl.ds(pl.multiple_of(index * strip, strip), strip)
        rows = token_ref[at, :]
        token_wide[at, :] = rows.astype(jnp.float32)
        total_ref[...] += lax.dot_general(
            rows, rows, (((0,), (0,)), ((), ())), preferred_element_type=jnp.float32
        )

    gram_own[...] = total_ref[...].reshape(owners, share, width)
    each_partner(
        lambda there, where: where_owner(there, lambda: part_copy(there, where, me).start())
    )

    each_partner(lambda there, where: ask_copy(there, where, there).wait_recv())
    asked[pl.ds(me, 1)] = wanted_ref[pl.ds(me, 1)]
    to_scalar = pltpu.make_async_copy(asked, asked_scalar, scalar_sem)
    to_scalar.start()
    to_scalar.wait()

    def collect(there, target, place):
        burst = math.gcd(capacity, 32)

        @pl.loop(0, capacity // burst)
        def _(index):
            first = pl.multiple_of(index * burst, burst)
            for row in range(burst):
                chosen = asked_scalar[there, 0, first + row]
                staged_wide[pl.ds(first + row, 1), :] = token_wide[pl.ds(chosen, 1), :]

        target[place] = staged_wide[...].astype(jnp.bfloat16)

    def serve(there, where):
        collect(there, staged, there)
        row_copy(there, where, my_place).start()

    each_partner(serve)
    collect(me, fetched, my_place)

    def reduce_part():
        gram_parts[pl.ds(me, 1)] = gram_own[pl.ds(me, 1)]
        each_partner(lambda there, where: part_copy(me, where, there).wait_recv())
        gram_whole[pl.ds(me, 1)] = jnp.sum(gram_parts[...], axis=0, keepdims=True)
        each_partner(lambda there, where: sum_copy(there, where, me).start())

    where_owner(me, reduce_part)

    host_count = start_ref.shape[0]
    row_host = lax.broadcasted_iota(jnp.int32, (host_count, group * capacity), 0) + 1

    def inner_products(index, halves):
        rows = fetched[pl.ds(index * group, group)].reshape(group * capacity, width)
        both = lax.dot_general(
            halves, rows, (((1,), (1,)), ((), ())), preferred_element_type=jnp.float32
        )
        code = code_ref[index]
        weight = CONFIDENCE_SCALE * (code % COUNT_SPAN).astype(jnp.float32)
        return rows, both[:host_count] + both[host_count:], row_host == code // COUNT_SPAN, weight

    def add_rows(masked, rows):
        out = jnp.dot(split_pair(masked), rows, preferred_element_type=jnp.float32)
        total_ref[...] += out[:host_count] + out[host_count:]

    def first_spread(vectors):
        halves = split_pair(vectors)
        total_ref[...] = jnp.zeros_like(total_ref)

        def arrive(index, source):
            where = {"shard": source, "sub": index}
            row_copy(source * inner + index, where, index * outer + source).wait_recv()

        def add_group(index):
            rows, product, own, weight = inner_products(index, halves)
            add_rows(jnp.where(own, (1.0 + weight) - weight * product, 0.0), rows)

        @pl.loop(0, inner - 1)
        def _(step):
            index = lax.rem(at_inner + 1 + step, inner)

            @pl.loop(0, outer)
            def _(source):
                arrive(index, source)

            add_group(index)

        @pl.loop(0, outer - 1)
        def _(step):
            arrive(at_inner, lax.rem(at_outer + 1 + step, outer))

        add_group(at_inner)
        return total_ref[...]

    def spread(vectors):
        halves = split_pair(vectors)
        total_ref[...] = jnp.zeros_like(total_ref)

        @pl.loop(0, inner, unroll=4)
        def _(index):
            rows, product, own, weight = inner_products(index, halves)
            add_rows(jnp.where(own, weight * product, 0.0), rows)

        return total_ref[...]

    def squares(vectors):
        halves = split_pair(vectors)

        def add(index, total):
            rows, product, own, weight = inner_products(index, halves)
            value = jnp.where(own, weight * product * product, 0.0)
            return total + jnp.sum(value, axis=1, keepdims=True)

        return lax.fori_loop(0, inner, add, jnp.zeros((host_count, 1), jnp.float32), unroll=4)

    def smooth(vectors):
        gram = gram_whole[...].reshape(width, width)
        return (
            jnp.dot(vectors, gram, precision=HIGHEST, preferred_element_type=jnp.float32)
            + RIDGE_WEIGHT * vectors
        )

    iterate = start_ref[...]
    residual = first_spread(iterate)
    each_partner(
        lambda there, where: where_owner(there, lambda: sum_copy(there, where, there).wait_recv())
    )
    residual = residual - smooth(iterate)
    direction = residual
    norm_now = jnp.sum(residual * residual, axis=1, keepdims=True)
    for iteration in range(CG_STEPS):
        image = smooth(direction)
        if iteration < CG_STEPS - 1:
            image = image + spread(direction)
            along = jnp.sum(direction * image, axis=1, keepdims=True)
        else:
            along = jnp.sum(direction * image, axis=1, keepdims=True) + squares(direction)
        step_size = norm_now / (along + SMALL_EPSILON)
        iterate = iterate + step_size * direction
        if iteration < CG_STEPS - 1:
            residual = residual - step_size * image
            norm_next = jnp.sum(residual * residual, axis=1, keepdims=True)
            direction = residual + norm_next / (norm_now + SMALL_EPSILON) * direction
            norm_now = norm_next
    out_ref[...] = iterate

    def settle(there, where):
        ask_copy(there, where, me).wait_send()
        where_owner(there, lambda: part_copy(there, where, me).wait_send())
        where_owner(me, lambda: sum_copy(there, where, me).wait_send())
        row_copy(there, where, my_place).wait_send()

    each_partner(settle)


def shards(host_factors, token_ids, counts, lengths, token_factors):
    outer, inner = lax.axis_size("shard"), lax.axis_size("sub")
    device_count = outer * inner
    token_rows = token_factors.shape[0]
    host_count, slot_count = token_ids.shape
    width = host_factors.shape[1]
    capacity = max(16, host_count * slot_count // device_count)
    share = max(8, width // device_count)
    owners = width // share
    wanted, codes = request_tables(
        token_ids, counts, lengths, token_rows, device_count, capacity
    )
    wanted = wanted.reshape(device_count, 1, capacity)
    codes = codes.reshape(outer, inner, capacity).transpose(1, 0, 2)
    codes = codes.reshape(inner, 1, outer * capacity)
    in_vmem = pl.BlockSpec(memory_space=pltpu.VMEM)
    links = [pltpu.SemaphoreType.DMA((device_count,))] * 8
    return pl.pallas_call(
        functools.partial(solve_body, (outer, inner, capacity)),
        out_shape=jax.ShapeDtypeStruct((host_count, width), jnp.float32),
        in_specs=[pl.BlockSpec(memory_space=pl.ANY)] + [in_vmem] * 3,
        out_specs=in_vmem,
        scratch_shapes=[
            pltpu.VMEM((token_rows, width), jnp.bfloat16),
            pltpu.VMEM((token_rows, width), jnp.float32),
            pltpu.VMEM((device_count, 1, capacity), jnp.int32),
            pltpu.SMEM((device_count, 1, capacity), jnp.int32),
            pltpu.VMEM((capacity, width), jnp.float32),
            pltpu.VMEM((device_count, capacity, width), jnp.bfloat16),
            pltpu.VMEM((device_count, capacity, width), jnp.bfloat16),
            pltpu.VMEM((owners, share, width), jnp.float32),
            pltpu.VMEM((device_count, share, width), jnp.float32),
            pltpu.VMEM((owners, share, width), jnp.float32),
            pltpu.VMEM((host_count, width), jnp.float32),
            pltpu.SemaphoreType.DMA,
            pltpu.SemaphoreType.DMA,
        ]
        + links,
        compiler_params=pltpu.CompilerParams(
            vmem_limit_bytes=48 * 1024 * 1024, collective_id=0, has_side_effects=True
        ),
    )(token_factors, wanted, codes, host_factors)


def solution(mesh):
    placed = (
        P(("parts", "shard", "sub"), None),
        P(("parts", "shard", "sub"), None),
        P(("parts", "shard", "sub"), None),
        P(("parts", "shard", "sub")),
        P(("parts", "shard", "sub"), None),
    )
    return jax.shard_map(
        shards,
        mesh=mesh,
        in_specs=placed,
        out_specs=P(("parts", "shard", "sub"), None),
        check_vma=False,
    )
```

```python
import functools
import math

import jax
import jax.numpy as jnp
from jax import lax
from jax.experimental import pallas as pl
from jax.experimental.pallas import tpu as pltpu
from jax.sharding import PartitionSpec as P

CG_STEPS = 3
CONFIDENCE_SCALE = 40.0
RIDGE_WEIGHT = 0.1
SMALL_EPSILON = 1e-06
HIGHEST = lax.Precision.HIGHEST
COUNT_SPAN = 64
DIGIT = 128


def owner_ranks(owner_hot, block_rows):
    total_rows, owner_width = owner_hot.shape
    block_count = total_rows // block_rows
    blocked = owner_hot.reshape(block_count, block_rows, owner_width)
    position = jnp.arange(block_rows, dtype=jnp.int32)
    lower_mask = (position[:, None] > position[None, :]).astype(jnp.bfloat16)
    within = jnp.einsum("ij,bjk->bik", lower_mask, blocked, preferred_element_type=jnp.float32)
    totals = jnp.sum(blocked.astype(jnp.float32), axis=1)
    block_index = jnp.arange(block_count, dtype=jnp.int32)
    block_lower = (block_index[:, None] > block_index[None, :]).astype(jnp.float32)
    before = jnp.dot(block_lower, totals, precision=HIGHEST)
    running = within + before[:, None, :]
    ranks = jnp.sum(running * blocked.astype(jnp.float32), axis=2)
    return ranks.reshape(total_rows).astype(jnp.int32)


def request_tables(token_ids, counts, lengths, token_rows, device_count, capacity):
    host_count, slot_count = token_ids.shape
    alive_mask = jnp.arange(slot_count, dtype=jnp.int32)[None, :] < lengths[:, None]
    owners = jnp.where(alive_mask, token_ids // token_rows, device_count).reshape(-1)
    local_rows = (token_ids % token_rows).reshape(-1)
    hosts = jnp.arange(host_count, dtype=jnp.int32)[:, None]
    codes = ((hosts + 1) * COUNT_SPAN + counts).reshape(-1)
    total_rows = host_count * slot_count
    block_rows = math.gcd(total_rows, 512)
    owner_hot = (owners[:, None] == jnp.arange(device_count + 1, dtype=jnp.int32)[None, :]).astype(
        jnp.bfloat16
    )
    ranks = owner_ranks(owner_hot, block_rows)
    capacity_index = jnp.arange(capacity, dtype=jnp.int32)

    digits = jnp.stack(
        [local_rows // DIGIT, local_rows % DIGIT, codes // DIGIT, codes % DIGIT], axis=1
    ).astype(jnp.bfloat16)
    valued = (digits[:, :, None] * owner_hot[:, None, :device_count]).reshape(
        total_rows, 4 * device_count
    )
    rank_hot = (ranks[:, None] == capacity_index[None, :]).astype(jnp.bfloat16)
    placed = lax.dot_general(
        valued, rank_hot, (((0,), (0,)), ((), ())), preferred_element_type=jnp.float32
    )
    placed = placed.astype(jnp.int32).reshape(4, device_count, capacity)
    return placed[0] * DIGIT + placed[1], placed[2] * DIGIT + placed[3]


def split_pair(values):
    high = values.astype(jnp.bfloat16)
    low = (values - high.astype(jnp.float32)).astype(jnp.bfloat16)
    return jnp.concatenate([high, low], axis=0)


def solve_body(
    sizes,
    token_home,
    wanted_ref,
    code_ref,
    start_ref,
    out_ref,
    token_ref,
    token_wide,
    asked,
    asked_scalar,
    staged_wide,
    staged,
    fetched,
    gram_own,
    gram_parts,
    gram_whole,
    total_ref,
    scalar_sem,
    token_sem,
    ask_send,
    ask_recv,
    part_send,
    part_recv,
    sum_send,
    sum_recv,
    row_send,
    row_recv,
):
    outer, inner, capacity = sizes
    group = outer
    count = outer * inner
    owners, share, width = gram_whole.shape
    at_outer, at_inner = lax.axis_index("shard"), lax.axis_index("sub")
    me = at_outer * inner + at_inner
    my_place = at_inner * outer + at_outer

    def partner(offset):
        there_outer = lax.rem(at_outer + lax.rem(offset, outer), outer)
        there_inner = lax.rem(at_inner + offset // outer, inner)
        return there_outer * inner + there_inner, {"shard": there_outer, "sub": there_inner}

    def each_partner(action):
        @pl.loop(0, count - 1)
        def _(step):
            action(*partner(count - 1 - step))

    def where_owner(device, action):
        if owners == count:
            action()
        else:
            pl.when(device < owners)(action)

    def ask_copy(there, where, slot):
        return pltpu.make_async_remote_copy(
            src_ref=wanted_ref.at[there],
            dst_ref=asked.at[slot],
            send_sem=ask_send.at[there],
            recv_sem=ask_recv.at[slot],
            device_id=where,
            device_id_type=pl.DeviceIdType.MESH,
        )

    def part_copy(there, where, slot):
        return pltpu.make_async_remote_copy(
            src_ref=gram_own.at[there],
            dst_ref=gram_parts.at[slot],
            send_sem=part_send.at[there],
            recv_sem=part_recv.at[slot],
            device_id=where,
            device_id_type=pl.DeviceIdType.MESH,
        )

    def sum_copy(there, where, slot):
        return pltpu.make_async_remote_copy(
            src_ref=gram_whole.at[slot],
            dst_ref=gram_whole.at[slot],
            send_sem=sum_send.at[there],
            recv_sem=sum_recv.at[slot],
            device_id=where,
            device_id_type=pl.DeviceIdType.MESH,
        )

    def row_copy(there, where, slot):
        return pltpu.make_async_remote_copy(
            src_ref=staged.at[there],
            dst_ref=fetched.at[slot],
            send_sem=row_send.at[there],
            recv_sem=row_recv.at[slot],
            device_id=where,
            device_id_type=pl.DeviceIdType.MESH,
        )

    bring = pltpu.make_async_copy(token_home, token_ref, token_sem)
    bring.start()
    barrier = pltpu.get_barrier_semaphore()
    each_partner(
        lambda there, where: pl.semaphore_signal(
            barrier, inc=1, device_id=where, device_id_type=pl.DeviceIdType.MESH
        )
    )
    pl.semaphore_wait(barrier, count - 1)
    each_partner(lambda there, where: ask_copy(there, where, me).start())

    total_ref[...] = jnp.zeros_like(total_ref)
    bring.wait()
    strip = math.gcd(token_ref.shape[0], 2048)

    @pl.loop(0, token_ref.shape[0] // strip)
    def _(index):
        at = pl.ds(pl.multiple_of(index * strip, strip), strip)
        rows = token_ref[at, :]
        token_wide[at, :] = rows.astype(jnp.float32)
        total_ref[...] += lax.dot_general(
            rows, rows, (((0,), (0,)), ((), ())), preferred_element_type=jnp.float32
        )

    gram_own[...] = total_ref[...].reshape(owners, share, width)
    each_partner(
        lambda there, where: where_owner(there, lambda: part_copy(there, where, me).start())
    )

    each_partner(lambda there, where: ask_copy(there, where, there).wait_recv())
    asked[pl.ds(me, 1)] = wanted_ref[pl.ds(me, 1)]
    to_scalar = pltpu.make_async_copy(asked, asked_scalar, scalar_sem)
    to_scalar.start()
    to_scalar.wait()

    def collect(there, target, place):
        burst = math.gcd(capacity, 32)

        @pl.loop(0, capacity // burst)
        def _(index):
            first = pl.multiple_of(index * burst, burst)
            for row in range(burst):
                chosen = asked_scalar[there, 0, first + row]
                staged_wide[pl.ds(first + row, 1), :] = token_wide[pl.ds(chosen, 1), :]

        target[place] = staged_wide[...].astype(jnp.bfloat16)

    def serve(there, where):
        collect(there, staged, there)
        row_copy(there, where, my_place).start()

    each_partner(serve)
    collect(me, fetched, my_place)

    def reduce_part():
        gram_parts[pl.ds(me, 1)] = gram_own[pl.ds(me, 1)]
        each_partner(lambda there, where: part_copy(me, where, there).wait_recv())
        gram_whole[pl.ds(me, 1)] = jnp.sum(gram_parts[...], axis=0, keepdims=True)
        each_partner(lambda there, where: sum_copy(there, where, me).start())

    where_owner(me, reduce_part)

    host_count = start_ref.shape[0]
    row_host = lax.broadcasted_iota(jnp.int32, (host_count, group * capacity), 0) + 1

    def inner_products(index, halves):
        rows = fetched[pl.ds(index * group, group)].reshape(group * capacity, width)
        both = lax.dot_general(
            halves, rows, (((1,), (1,)), ((), ())), preferred_element_type=jnp.float32
        )
        code = code_ref[index]
        weight = CONFIDENCE_SCALE * (code % COUNT_SPAN).astype(jnp.float32)
        return rows, both[:host_count] + both[host_count:], row_host == code // COUNT_SPAN, weight

    def add_rows(masked, rows):
        out = jnp.dot(split_pair(masked), rows, preferred_element_type=jnp.float32)
        total_ref[...] += out[:host_count] + out[host_count:]

    def first_spread(vectors):
        halves = split_pair(vectors)
        total_ref[...] = jnp.zeros_like(total_ref)

        def arrive(index, source):
            where = {"shard": source, "sub": index}
            row_copy(source * inner + index, where, index * outer + source).wait_recv()

        def add_group(index):
            rows, product, own, weight = inner_products(index, halves)
            add_rows(jnp.where(own, (1.0 + weight) - weight * product, 0.0), rows)

        @pl.loop(0, inner - 1)
        def _(step):
            index = lax.rem(at_inner + 1 + step, inner)

            @pl.loop(0, outer)
            def _(source):
                arrive(index, source)

            add_group(index)

        @pl.loop(0, outer - 1)
        def _(step):
            arrive(at_inner, lax.rem(at_outer + 1 + step, outer))

        add_group(at_inner)
        return total_ref[...]

    def spread(vectors):
        halves = split_pair(vectors)

        def add(index, total):
            rows, product, own, weight = inner_products(index, halves)
            masked = split_pair(jnp.where(own, weight * product, 0.0))
            out = jnp.dot(masked, rows, preferred_element_type=jnp.float32)
            return total + (out[:host_count] + out[host_count:])

        return lax.fori_loop(0, inner, add, jnp.zeros((host_count, width), jnp.float32), unroll=4)

    def squares(vectors):
        halves = split_pair(vectors)

        def add(index, total):
            rows, product, own, weight = inner_products(index, halves)
            value = jnp.where(own, weight * product * product, 0.0)
            return total + jnp.sum(value, axis=1, keepdims=True)

        return lax.fori_loop(0, inner, add, jnp.zeros((host_count, 1), jnp.float32), unroll=4)

    def smooth(vectors):
        gram = gram_whole[...].reshape(width, width)
        return (
            jnp.dot(vectors, gram, precision=HIGHEST, preferred_element_type=jnp.float32)
            + RIDGE_WEIGHT * vectors
        )

    iterate = start_ref[...]
    residual = first_spread(iterate)
    each_partner(
        lambda there, where: where_owner(there, lambda: sum_copy(there, where, there).wait_recv())
    )
    residual = residual - smooth(iterate)
    direction = residual
    norm_now = jnp.sum(residual * residual, axis=1, keepdims=True)
    for iteration in range(CG_STEPS):
        image = smooth(direction)
        if iteration < CG_STEPS - 1:
            image = image + spread(direction)
            along = jnp.sum(direction * image, axis=1, keepdims=True)
        else:
            along = jnp.sum(direction * image, axis=1, keepdims=True) + squares(direction)
        step_size = norm_now / (along + SMALL_EPSILON)
        iterate = iterate + step_size * direction
        if iteration < CG_STEPS - 1:
            residual = residual - step_size * image
            norm_next = jnp.sum(residual * residual, axis=1, keepdims=True)
            direction = residual + norm_next / (norm_now + SMALL_EPSILON) * direction
            norm_now = norm_next
    out_ref[...] = iterate

    def settle(there, where):
        ask_copy(there, where, me).wait_send()
        where_owner(there, lambda: part_copy(there, where, me).wait_send())
        where_owner(me, lambda: sum_copy(there, where, me).wait_send())
        row_copy(there, where, my_place).wait_send()

    each_partner(settle)


def shards(host_factors, token_ids, counts, lengths, token_factors):
    outer, inner = lax.axis_size("shard"), lax.axis_size("sub")
    device_count = outer * inner
    token_rows = token_factors.shape[0]
    host_count, slot_count = token_ids.shape
    width = host_factors.shape[1]
    capacity = max(16, host_count * slot_count // device_count)
    share = max(8, width // device_count)
    owners = width // share
    wanted, codes = request_tables(
        token_ids, counts, lengths, token_rows, device_count, capacity
    )
    wanted = wanted.reshape(device_count, 1, capacity)
    codes = codes.reshape(outer, inner, capacity).transpose(1, 0, 2)
    codes = codes.reshape(inner, 1, outer * capacity)
    in_vmem = pl.BlockSpec(memory_space=pltpu.VMEM)
    links = [pltpu.SemaphoreType.DMA((device_count,))] * 8
    return pl.pallas_call(
        functools.partial(solve_body, (outer, inner, capacity)),
        out_shape=jax.ShapeDtypeStruct((host_count, width), jnp.float32),
        in_specs=[pl.BlockSpec(memory_space=pl.ANY)] + [in_vmem] * 3,
        out_specs=in_vmem,
        scratch_shapes=[
            pltpu.VMEM((token_rows, width), jnp.bfloat16),
            pltpu.VMEM((token_rows, width), jnp.float32),
            pltpu.VMEM((device_count, 1, capacity), jnp.int32),
            pltpu.SMEM((device_count, 1, capacity), jnp.int32),
            pltpu.VMEM((capacity, width), jnp.float32),
            pltpu.VMEM((device_count, capacity, width), jnp.bfloat16),
            pltpu.VMEM((device_count, capacity, width), jnp.bfloat16),
            pltpu.VMEM((owners, share, width), jnp.float32),
            pltpu.VMEM((device_count, share, width), jnp.float32),
            pltpu.VMEM((owners, share, width), jnp.float32),
            pltpu.VMEM((host_count, width), jnp.float32),
            pltpu.SemaphoreType.DMA,
            pltpu.SemaphoreType.DMA,
        ]
        + links,
        compiler_params=pltpu.CompilerParams(
            vmem_limit_bytes=48 * 1024 * 1024, collective_id=0, has_side_effects=True
        ),
    )(token_factors, wanted, codes, host_factors)


def solution(mesh):
    placed = (
        P(("parts", "shard", "sub"), None),
        P(("parts", "shard", "sub"), None),
        P(("parts", "shard", "sub"), None),
        P(("parts", "shard", "sub")),
        P(("parts", "shard", "sub"), None),
    )
    return jax.shard_map(
        shards,
        mesh=mesh,
        in_specs=placed,
        out_specs=P(("parts", "shard", "sub"), None),
        check_vma=False,
    )
```
